32 devices in a mesh: ctx: 8 (over z, x), head: 4 (over y, core).
Axes of the slice: x: 2, y: 2, z: 4, core: 2. Of those that a mesh axis runs over, the one named last changes fastest.
Arguments:
- queries: bfloat16 [4096, 2048], P('ctx', 'head'), may hold values from -6 to 6
- key_states: bfloat16 [4096, 256], P('ctx', 'head'), may hold values from -6 to 6
- value_states: bfloat16 [4096, 256], P('ctx', 'head'), may hold values from -6 to 6
- attn_out: bfloat16 [4096, 2048], P('ctx', 'head'), may hold values from -2 to 2
- grad_out: bfloat16 [4096, 2048], P('ctx', 'head'), may hold values from -6 to 6
- log_norm: float32 [16, 4096], P('head', 'ctx'), as said below
- doc_lengths: int32 [16], replicated, may hold values from 1 to 2048, as said below
Outputs:
- grad_queries: bfloat16 [4096, 2048], P('ctx', 'head')
- grad_keys: bfloat16 [4096, 256], P('ctx', 'head')
- grad_values: bfloat16 [4096, 256], P('ctx', 'head')
The draws below stay inside these ranges and needn't reach their ends.
Inputs may be any that keep to these rules, and one draw needn't show every extreme that they name: `doc_lengths`: 16 document lengths that add up to 4096; one document has exactly 2048 tokens. `log_norm`: a given input, not recomputed from the others.
All inputs are finite; a program needn't handle non-finite values.
Results may differ from the reference program's by a relative error of at most 0.0051.
Values may be sent and summed in bfloat16 or wider, within the bound.
No kernel may reach another device: no remote copies, remote signals or barrier semaphores. Data moves between devices by JAX's collectives and lax.ppermute only.
A program may use at most 64 MiB of HBM per device.

```python
import jax
import jax.numpy as jnp
from jax import lax

DH = 128
GROUP = 8
QH = 16
KVH = 2
TOK_DEV = 512
TOKENS = 4096
MOST = 2048
NDOCS = 16


def doc_cuts(key):
    folded = jax.random.fold_in(key, 11)
    key_offset, key_rank, key_guard = jax.random.split(folded, 3)
    groups = TOKENS // MOST
    offset = jax.random.randint(key_offset, (), 1, MOST).astype(jnp.int32)
    chosen = jax.random.randint(key_guard, (), 0, groups - 1).astype(jnp.int32)
    guarded = offset + MOST * chosen
    places = jnp.arange(TOKENS, dtype=jnp.int32)
    lattice = offset + MOST * jnp.arange(groups, dtype=jnp.int32)
    inside = (places > guarded) & (places < guarded + MOST)
    allowed = (places >= 1) & ((places - offset) % MOST != 0) & jnp.logical_not(inside)
    random_rank = jax.random.randint(key_rank, (TOKENS,), 0, 16384).astype(jnp.int32)
    scores = jnp.where(allowed, random_rank * TOKENS + places, -1 - places)
    picked = lax.top_k(scores, NDOCS - groups - 1)[1].astype(jnp.int32)
    cut_points = jnp.sort(jnp.concatenate([lattice, picked]))
    bounds = jnp.concatenate([jnp.zeros((1,), jnp.int32), cut_points, jnp.full((1,), TOKENS, jnp.int32)])
    return (bounds[1:] - bounds[:-1]).astype(jnp.int32)


def draw_doc_lengths(key, part):
    return doc_cuts(key)


def draw_log_norm(key, part):
    lengths = doc_cuts(key)
    doc_ends = jnp.cumsum(lengths).astype(jnp.int32)
    places = jnp.arange(TOKENS, dtype=jnp.int32)
    starts = jnp.sum(jnp.where(doc_ends[None, :] <= places[:, None], lengths[None, :], 0), axis=1)
    counts = (places - starts + 1).astype(jnp.float32)
    noise_key = jax.random.fold_in(key, 23)
    spread = jax.random.uniform(noise_key, (QH, TOKENS), jnp.float32)
    level = 0.5 + spread
    return (jnp.log(counts)[None, :] + level).astype(jnp.float32)


def levels(rng, shape, cuts, least, top_value):
    def one(axis_at, blocks):
        draws = jax.random.uniform(jax.random.fold_in(jax.random.fold_in(rng, 6), axis_at), (blocks,), jnp.float32, least / len(cuts), top_value / len(cuts))
        return jnp.repeat(jnp.exp(draws), shape[axis_at] // blocks).reshape((-1,) + (1,) * (len(shape) - axis_at - 1))

    factor_of = one(*cuts[0])
    for cut in cuts[1:]:
        factor_of = factor_of * one(*cut)
    return factor_of


def normal_values(stream_key, extent, scale, limit, cuts=(), kind=jnp.bfloat16):
    drawn = jax.random.normal(stream_key, extent, jnp.float32) * scale
    if len(cuts) > 0:
        drawn = levels(stream_key, extent, cuts, -0.22, 0.18) * drawn
    return jnp.clip(drawn, min=-limit, max=limit).astype(kind)


def setup_inputs(seed: int = 0) -> dict:
    splits = jax.random.split(jax.random.key(seed), 8)
    queries = normal_values(splits[0], (TOKENS, QH * DH), 1.0, 6.0, ((0, 8), (1, 4)))
    key_states = normal_values(splits[1], (TOKENS, KVH * DH), 1.0, 6.0, ((0, 8), (1, 4)))
    value_states = normal_values(splits[2], (TOKENS, KVH * DH), 1.0, 6.0, ((0, 8), (1, 4)))
    attn_out = normal_values(splits[3], (TOKENS, QH * DH), 0.3, 2.0, ((0, 8), (1, 4)))
    grad_out = normal_values(splits[4], (TOKENS, QH * DH), 1.0, 6.0, ((0, 8), (1, 4)))
    log_norm = draw_log_norm(jax.random.fold_in(splits[7], 71), 0)
    doc_lengths = draw_doc_lengths(jax.random.fold_in(splits[7], 71), 0)
    return dict(queries=queries, key_states=key_states, value_states=value_states, attn_out=attn_out, grad_out=grad_out, log_norm=log_norm, doc_lengths=doc_lengths)


def reference(queries, key_states, value_states, attn_out, grad_out, log_norm, doc_lengths):
    score_scale = DH ** -0.5
    tile_rows = min(512, TOK_DEV)
    block_count = TOKENS // tile_rows
    window_len = MOST + tile_rows
    places = jnp.arange(TOKENS, dtype=jnp.int32)
    doc_ends = jnp.cumsum(doc_lengths).astype(jnp.int32)
    starts = jnp.sum(jnp.where(doc_ends[None, :] <= places[:, None], doc_lengths[None, :], 0), axis=1).astype(jnp.int32)
    query_heads = queries.astype(jnp.float32).reshape(TOKENS, KVH, GROUP, DH)
    grad_heads = grad_out.astype(jnp.float32).reshape(TOKENS, KVH, GROUP, DH)
    row_delta = jnp.sum((attn_out.astype(jnp.float32) * grad_out.astype(jnp.float32)).reshape(TOKENS, QH, DH), axis=-1)
    row_delta = row_delta.reshape(TOKENS, KVH, GROUP)
    norm_heads = jnp.transpose(log_norm).reshape(TOKENS, KVH, GROUP)
    front = jnp.zeros((MOST, KVH, DH), jnp.float32)
    key_padded = jnp.concatenate([front, key_states.astype(jnp.float32).reshape(TOKENS, KVH, DH)], axis=0)
    value_padded = jnp.concatenate([front, value_states.astype(jnp.float32).reshape(TOKENS, KVH, DH)], axis=0)
    high = lax.Precision.HIGHEST

    def one_block(carried, block_index):
        key_grads, value_grads = carried
        first_row = (block_index * tile_rows).astype(jnp.int32)
        tile_queries = lax.dynamic_slice_in_dim(query_heads, first_row, tile_rows, 0)
        tile_grads = lax.dynamic_slice_in_dim(grad_heads, first_row, tile_rows, 0)
        tile_norm = jnp.transpose(lax.dynamic_slice_in_dim(norm_heads, first_row, tile_rows, 0), (1, 2, 0))
        tile_delta = jnp.transpose(lax.dynamic_slice_in_dim(row_delta, first_row, tile_rows, 0), (1, 2, 0))
        query_pos = first_row + jnp.arange(tile_rows, dtype=jnp.int32)
        query_start = lax.dynamic_slice_in_dim(starts, first_row, tile_rows, 0)
        tile_keys = lax.dynamic_slice_in_dim(key_padded, first_row, window_len, 0)
        tile_values = lax.dynamic_slice_in_dim(value_padded, first_row, window_len, 0)
        key_pos = first_row - MOST + jnp.arange(window_len, dtype=jnp.int32)
        allowed = (key_pos[None, :] <= query_pos[:, None]) & (key_pos[None, :] >= query_start[:, None])
        scores = jnp.einsum('qagd,kad->agqk', tile_queries, tile_keys, precision=high) * score_scale
        probs = jnp.where(allowed[None, None], jnp.exp(scores - tile_norm[..., None]), jnp.float32(0.0))
        dprobs = jnp.einsum('qagd,kad->agqk', tile_grads, tile_values, precision=high)
        dscores = probs * (dprobs - tile_delta[..., None])
        probs_b = lax.optimization_barrier(probs.astype(jnp.bfloat16)).astype(jnp.float32)
        dscores_b = lax.optimization_barrier(dscores.astype(jnp.bfloat16)).astype(jnp.float32)
        value_part = jnp.einsum('agqk,qagd->kad', probs_b, tile_grads, precision=high)
        key_part = jnp.einsum('agqk,qagd->kad', dscores_b, tile_queries, precision=high)
        query_part = jnp.einsum('agqk,kad->qagd', dscores_b, tile_keys, precision=high)
        previous = lax.dynamic_slice_in_dim(key_grads, first_row, window_len, 0)
        key_grads = lax.dynamic_update_slice_in_dim(key_grads, previous + key_part, first_row, 0)
        previous = lax.dynamic_slice_in_dim(value_grads, first_row, window_len, 0)
        value_grads = lax.dynamic_update_slice_in_dim(value_grads, previous + value_part, first_row, 0)
        return (key_grads, value_grads), query_part

    empty = jnp.zeros((MOST + TOKENS, KVH, DH), jnp.float32)
    (key_grads, value_grads), query_parts = lax.scan(one_block, (empty, empty), jnp.arange(block_count, dtype=jnp.int32))
    grad_queries = (query_parts.reshape(TOKENS, QH * DH) * score_scale).astype(jnp.bfloat16)
    grad_keys = (key_grads[MOST:].reshape(TOKENS, KVH * DH) * score_scale).astype(jnp.bfloat16)
    grad_values = value_grads[MOST:].reshape(TOKENS, KVH * DH).astype(jnp.bfloat16)
    return (grad_queries, grad_keys, grad_values)
```

```python
import functools

import jax
import jax.numpy as jnp
from jax import lax
from jax.experimental import pallas as pl
from jax.experimental.pallas import tpu as pltpu
from jax.sharding import PartitionSpec as P

SPAN = 4
TILE = 256
LOG2E = 1.4426950408889634
NT = (((1,), (1,)), ((), ()))


def partner(value):
    count = lax.axis_size("head")
    return lax.ppermute(value, "head", [(i, i ^ 1) for i in range(count)])


def passed_along(value, by):
    count = lax.axis_size("ctx")
    pairs = [(i, i + by) for i in range(count) if 0 <= i + by < count]
    return lax.ppermute(value, "ctx", pairs)


def dot(a, b, dims=(((1,), (0,)), ((), ()))):
    return lax.dot_general(a, b, dims, preferred_element_type=jnp.float32)


def joined(lower, upper, half):
    keys = jnp.concatenate([lower[:, :half], upper[:, :half]], axis=1)
    values = jnp.concatenate([lower[:, half:], upper[:, half:]], axis=1)
    return keys, values


def row_start(docs, position):
    def step(j, state):
        total, found = state
        total = total + docs[j]
        return total, jnp.where(total <= position, total, found)

    zero = jnp.int32(0)
    return lax.fori_loop(0, docs.shape[0], step, (zero, zero), unroll=True)[1]


def row_starts(docs, positions):
    def step(j, state):
        total, found = state
        total = total + docs[j]
        return total, jnp.where(positions >= total, total, found)

    start = (jnp.int32(0), jnp.zeros_like(positions))
    return lax.fori_loop(0, docs.shape[0], step, start, unroll=True)[1]


def block_kernel(distances, first, scale, place, docs, q, g, norms, extra, *rest):
    blocks = len(distances)
    rest = list(rest)
    prior = None if first else rest.pop(0)
    mine, other, rest = rest[:blocks], rest[blocks : 2 * blocks], rest[2 * blocks :]
    if first:
        query_out, delta_ref, kept, sent, keys, keys_t, values, starts_ref, dk, dv = rest
        dq = query_out
    else:
        query_out, kept, sent, keys, keys_t, values, starts_ref, dk, dv, dq = rest
        delta_ref = extra
    rows = q.shape[0]
    heads, size = norms.shape[0], q.shape[1] // norms.shape[0]
    half = size // 2
    ctx_index, upper = place[0], place[1] == 1
    first_pos = ctx_index * rows

    positions = first_pos + lax.broadcasted_iota(jnp.int32, (1, rows), 1)
    starts_ref[...] = row_starts(docs, positions)
    lowest = [row_start(docs, first_pos + t * TILE) for t in range(rows // TILE)]
    lowest_start = lowest[0]

    if first:
        ones = jnp.ones((8, size), jnp.bfloat16)
        for h in range(heads):
            cols = slice(h * size, (h + 1) * size)
            product = extra[:, cols].astype(jnp.float32) * g[:, cols].astype(jnp.float32)
            high = product.astype(jnp.bfloat16)
            low = (product - high.astype(jnp.float32)).astype(jnp.bfloat16)
            total = dot(ones, high, NT) + dot(ones, low, NT)
            delta_ref[h : h + 1, :] = total[:1, :]
        dq[...] = jnp.zeros_like(dq)
    else:
        dq[...] = prior[...]

    for j, distance in enumerate(distances):
        block_needed = (ctx_index >= distance) & (
            (ctx_index - distance + 1) * rows > lowest_start
        )
        span = slice(j * rows, (j + 1) * rows)

        @pl.when(block_needed)
        def _(j=j, span=span):
            a, b = mine[j][...], other[j][...]
            lower = jnp.where(upper, b, a)
            above = jnp.where(upper, a, b)
            k, v = joined(lower, above, half)
            keys[span, :] = k
            values[span, :] = v
            keys_t[:, span] = k.T

    def key_tile(index, carry):
        block = index // (rows // TILE)
        distance = distances[0] + block
        base = pl.multiple_of(index * TILE, TILE)
        key_lo = (ctx_index - distance) * rows + (index % (rows // TILE)) * TILE
        dk[...] = jnp.zeros_like(dk)
        dv[...] = jnp.zeros_like(dv)
        for t in range(rows // TILE):
            query_lo = first_pos + t * TILE
            needed = (
                (ctx_index >= distance)
                & (key_lo <= query_lo + TILE - 1)
                & (key_lo + TILE - 1 >= lowest[t])
            )

            @pl.when(needed)
            def _(t=t, query_lo=query_lo):
                k = keys[pl.ds(base, TILE), :]
                v = values[pl.ds(base, TILE), :]
                kt = keys_t[:, pl.ds(base, TILE)]
                lanes = slice(t * TILE, (t + 1) * TILE)
                key_pos = key_lo + lax.broadcasted_iota(jnp.int32, (TILE, TILE), 0)
                query_pos = query_lo + lax.broadcasted_iota(jnp.int32, (TILE, TILE), 1)
                allowed = (key_pos <= query_pos) & (key_pos >= starts_ref[:, lanes])
                key_sum, value_sum = dk[...], dv[...]
                for h in range(heads):
                    cols = slice(h * size, (h + 1) * size)
                    qh, gh = q[lanes, cols], g[lanes, cols]
                    level = norms[h : h + 1, lanes] * LOG2E
                    delta = delta_ref[h : h + 1, lanes]
                    scores = dot(k, qh, NT) * (scale * LOG2E)
                    probs = jnp.where(allowed, jnp.exp2(scores - level), 0.0)
                    dscores = probs * (dot(v, gh, NT) - delta)
                    probs = probs.astype(jnp.bfloat16)
                    dscores = dscores.astype(jnp.bfloat16)
                    value_sum = value_sum + dot(probs, gh)
                    key_sum = key_sum + dot(dscores, qh)
                    dq[cols, lanes] += dot(kt, dscores)
                dk[...] = key_sum
                dv[...] = value_sum

        key_sum, value_sum = dk[...], dv[...]
        lower = jnp.concatenate([key_sum[:, :half], value_sum[:, :half]], axis=1)
        above = jnp.concatenate([key_sum[:, half:], value_sum[:, half:]], axis=1)
        kept[pl.ds(base, TILE), :] = jnp.where(upper, above, lower)
        sent[pl.ds(base, TILE), :] = jnp.where(upper, lower, above).astype(sent.dtype)
        return carry

    lax.fori_loop(0, blocks * rows // TILE, key_tile, 0)

    if not first:
        for h in range(heads):
            cols = slice(h * size, (h + 1) * size)
            query_out[:, cols] = (dq[cols, :] * scale).T.astype(query_out.dtype)


def block_call(distances, first, place, docs, q, g, norms, extra, prior, mine, other):
    rows, width = q.shape
    heads = norms.shape[0]
    size = width // heads
    total = len(distances) * rows
    scale = size ** (-0.5)
    smem = pl.BlockSpec(memory_space=pltpu.SMEM)
    vmem = pl.BlockSpec(memory_space=pltpu.VMEM)
    operands = [q, g, norms, extra] + ([] if first else [prior]) + mine + other
    partials = [
        jax.ShapeDtypeStruct((total, size), jnp.float32),
        jax.ShapeDtypeStruct((total, size), jnp.bfloat16),
    ]
    if first:
        outs = [
            jax.ShapeDtypeStruct((width, rows), jnp.float32),
            jax.ShapeDtypeStruct((heads, rows), jnp.float32),
        ] + partials
    else:
        outs = [jax.ShapeDtypeStruct((rows, width), jnp.bfloat16)] + partials
    scratch = [
        pltpu.VMEM((total, size), jnp.bfloat16),
        pltpu.VMEM((size, total), jnp.bfloat16),
        pltpu.VMEM((total, size), jnp.bfloat16),
        pltpu.VMEM((1, rows), jnp.int32),
        pltpu.VMEM((TILE, size), jnp.float32),
        pltpu.VMEM((TILE, size), jnp.float32),
    ]
    if not first:
        scratch.append(pltpu.VMEM((width, rows), jnp.float32))
    return pl.pallas_call(
        functools.partial(block_kernel, distances, first, scale),
        out_shape=outs,
        in_specs=[smem, smem] + [vmem] * len(operands),
        out_specs=[vmem] * len(outs),
        scratch_shapes=scratch,
        compiler_params=pltpu.CompilerParams(vmem_limit_bytes=32 * 1024 * 1024),
    )(place, docs, *operands)


def local(queries, key_states, value_states, attn_out, grad_out, log_norm, doc_lengths):
    half = key_states.shape[1]
    scale = (2 * half) ** (-0.5)
    place = jnp.stack([lax.axis_index("ctx"), lax.axis_index("head") % 2]).astype(jnp.int32)
    own = jnp.concatenate([key_states, value_states], axis=1)
    own_other = partner(own)
    arrived = [passed_along(own, d) for d in range(1, SPAN + 1)]
    arrived_other = [partner(a) for a in arrived]

    dq, delta, own_kept, own_sent = block_call(
        (0,), True, place, doc_lengths, queries, grad_out, log_norm, attn_out, None, [own], [own_other]
    )
    grad_queries, far_kept, far_sent = block_call(
        tuple(range(1, SPAN + 1)),
        False,
        place,
        doc_lengths,
        queries,
        grad_out,
        log_norm,
        delta,
        dq,
        arrived,
        arrived_other,
    )
    total = own_kept + partner(own_sent).astype(jnp.float32)
    far = (far_kept + partner(far_sent).astype(jnp.float32)).astype(jnp.bfloat16)
    rows = queries.shape[0]
    for d in range(1, SPAN + 1):
        total = total + passed_along(far[(d - 1) * rows : d * rows], -d).astype(jnp.float32)
    grad_keys = (total[:, :half] * scale).astype(jnp.bfloat16)
    grad_values = total[:, half:].astype(jnp.bfloat16)
    return grad_queries, grad_keys, grad_values


def solution(mesh):
    in_specs = (
        P("ctx", "head"),
        P("ctx", "head"),
        P("ctx", "head"),
        P("ctx", "head"),
        P("ctx", "head"),
        P("head", "ctx"),
        P(),
    )
    out_specs = (P("ctx", "head"), P("ctx", "head"), P("ctx", "head"))
    return jax.shard_map(local, mesh=mesh, in_specs=in_specs, out_specs=out_specs, check_vma=False)
```

```python
import functools

import jax
import jax.numpy as jnp
from jax import lax
from jax.experimental import pallas as pl
from jax.experimental.pallas import tpu as pltpu
from jax.sharding import PartitionSpec as P

STAGES = ((4, 3), (2, 1))
SWAP = True
RELAY = True
TIE = False
TILE = 256
LOG2E = 1.4426950408889634
NN = (((1,), (0,)), ((), ()))
NT = (((1,), (1,)), ((), ()))


def partner(value):
    count = lax.axis_size("head")
    return lax.ppermute(value, "head", [(i, i ^ 1) for i in range(count)])


def passed_along(value, by, parity=None):
    count = lax.axis_size("ctx")
    pairs = [(i, i + by) for i in range(count) if 0 <= i + by < count]
    if parity is not None:
        pairs = [pair for pair in pairs if pair[0] % 2 == parity]
    if SWAP and 2 * abs(by) == count:
        pairs += [(j, i) for i, j in pairs]
    return lax.ppermute(value, "ctx", pairs)


def neighbour(value):
    count = lax.axis_size("ctx")
    return lax.ppermute(value, "ctx", [(i, i ^ 1) for i in range(count)])


def dot(a, b, dims=NN):
    return lax.dot_general(a, b, dims, preferred_element_type=jnp.float32)


def row_start(docs, position):
    def step(j, state):
        total, found = state
        total = total + docs[j]
        return total, jnp.where(total <= position, total, found)

    zero = jnp.int32(0)
    return lax.fori_loop(0, docs.shape[0], step, (zero, zero), unroll=True)[1]


def row_starts(docs, positions):
    def step(j, state):
        total, found = state
        total = total + docs[j]
        return total, jnp.where(positions >= total, total, found)

    start = (jnp.int32(0), jnp.zeros_like(positions))
    return lax.fori_loop(0, docs.shape[0], step, start, unroll=True)[1]


def prepare_rows(first_pos, docs, g, norms, attn_out, facts, tiles, heads, size):
    rows = tiles * TILE
    positions = first_pos + lax.broadcasted_iota(jnp.int32, (1, rows), 1)
    starts = row_starts(docs, positions).astype(jnp.float32)
    positions = positions.astype(jnp.float32)
    ones = jnp.ones((8, size), jnp.bfloat16)
    for h in range(heads):
        cols = slice(h * size, (h + 1) * size)
        product = attn_out[:, cols].astype(jnp.float32) * g[:, cols].astype(jnp.float32)
        high = product.astype(jnp.bfloat16)
        low = (product - high.astype(jnp.float32)).astype(jnp.bfloat16)
        delta = (dot(ones, high, NT) + dot(ones, low, NT))[:1, :]
        level = norms[h : h + 1, :] * LOG2E
        for t in range(tiles):
            span = slice((t * heads + h) * TILE, (t * heads + h + 1) * TILE)
            part = slice(t * TILE, (t + 1) * TILE)
            facts[0:1, span] = level[:, part]
            facts[1:2, span] = delta[:, part]
            facts[2:3, span] = starts[:, part]
            facts[3:4, span] = positions[:, part]


def block_kernel(distances, first, heads, scale, place, docs, qt, gt, *rest):
    blocks = len(distances)
    rest = list(rest)
    if first:
        norms, attn_hbm = rest.pop(0), rest.pop(0)
    else:
        facts, prior = rest.pop(0), rest.pop(0)
    mine, other, rest = rest[:blocks], rest[blocks : 2 * blocks], rest[2 * blocks :]
    query_out = rest.pop(0)
    if first:
        facts = rest.pop(0)
        q_hbm, g_hbm, qt, gt = qt, gt, rest.pop(0), rest.pop(0)
    kept, sent, keys, keys_t, values, dk, dv = rest[:7]
    dq = query_out
    if first:
        attn_out, q, g, sems = rest[7:]
        pairs = ((attn_hbm, attn_out), (g_hbm, g), (q_hbm, q))
        loads = [pltpu.make_async_copy(a, b, sems.at[i]) for i, (a, b) in enumerate(pairs)]
        for load in loads:
            load.start()
    size, rows = qt.shape[0], qt.shape[1] // heads
    half = size // 2
    tiles = rows // TILE
    wide = heads * TILE
    ctx_index, upper = place[0], place[1] == 1
    first_pos = ctx_index * rows
    lowest = [row_start(docs, first_pos + t * TILE) for t in range(tiles)]
    highest = [row_start(docs, first_pos + (t + 1) * TILE - 1) for t in range(tiles)]

    if first:
        for load in loads:
            load.wait()
        prepare_rows(first_pos, docs, g, norms, attn_out, facts, tiles, heads, size)
        for t in range(tiles):
            for h in range(heads):
                span = slice((t * heads + h) * TILE, (t * heads + h + 1) * TILE)
                part = slice(t * TILE, (t + 1) * TILE)
                cols = slice(h * size, (h + 1) * size)
                qt[:, span] = q[part, cols].T
                gt[:, span] = g[part, cols].T
        dq[...] = jnp.zeros_like(dq)

    for j, distance in enumerate(distances):
        block_lo = (ctx_index - distance) * rows
        block_needed = (ctx_index >= distance) & (block_lo + rows > lowest[0])
        span = slice(j * rows, (j + 1) * rows)

        @pl.when(block_needed)
        def _(j=j, span=span, block_lo=block_lo):
            a, b = mine[j][...], other[j][...]
            lower = jnp.where(upper, b, a)
            above = jnp.where(upper, a, b)
            key_rows = jnp.concatenate([lower[:half, :], above[:half, :]], axis=0)
            value_rows = jnp.concatenate([lower[half:, :], above[half:, :]], axis=0)
            keys_t[...] = key_rows
            keys[...] = key_rows.T
            values[...] = value_rows.T

            def key_tile(index, carry):
                base = pl.multiple_of(index * TILE, TILE)
                key_lo = block_lo + base
                dk[...] = jnp.zeros_like(dk)
                dv[...] = jnp.zeros_like(dv)

                def query_tile(t, inner):
                    query_lo = first_pos + t * TILE
                    least, top = lowest[0], highest[0]
                    for other_t in range(1, tiles):
                        least = jnp.where(t == other_t, lowest[other_t], least)
                        top = jnp.where(t == other_t, highest[other_t], top)
                    needed = (key_lo <= query_lo + TILE - 1) & (key_lo + TILE - 1 >= least)

                    inside = (key_lo + TILE - 1 <= query_lo) & (key_lo >= top)

                    def tile(masked):
                        k = keys[pl.ds(base, TILE), :]
                        v = values[pl.ds(base, TILE), :]
                        kt = keys_t[:, pl.ds(base, TILE)]
                        lanes = pl.ds(pl.multiple_of(t * wide, wide), wide)
                        qs, gs = qt[:, lanes], gt[:, lanes]
                        scores = dot(k, qs) * (scale * LOG2E)
                        probs = jnp.exp2(scores - facts[0:1, lanes])
                        if masked:
                            offset = lax.broadcasted_iota(jnp.int32, (TILE, wide), 0)
                            offset = offset.astype(jnp.float32)
                            shift = key_lo.astype(jnp.float32)
                            allowed = (offset <= facts[3:4, lanes] - shift) & (
                                offset >= facts[2:3, lanes] - shift
                            )
                            probs = jnp.where(allowed, probs, 0.0)
                        dscores = probs * (dot(v, gs) - facts[1:2, lanes])
                        probs = probs.astype(jnp.bfloat16)
                        dscores = dscores.astype(jnp.bfloat16)
                        dv[...] += dot(gs, probs, NT)
                        dk[...] += dot(qs, dscores, NT)
                        dq[:, lanes] += dot(kt, dscores)

                    pl.when(inside)(functools.partial(tile, False))
                    pl.when(needed & jnp.logical_not(inside))(functools.partial(tile, True))

                    return inner

                lax.fori_loop(0, tiles, query_tile, 0)
                key_sum, value_sum = dk[...], dv[...]
                lower = jnp.concatenate([key_sum[:half], value_sum[:half]], axis=0)
                above = jnp.concatenate([key_sum[half:], value_sum[half:]], axis=0)
                out = pl.ds(pl.multiple_of(j * rows + base, TILE), TILE)
                kept[:, out] = jnp.where(upper, above, lower)
                sent[:, out] = jnp.where(upper, lower, above).astype(sent.dtype)
                return carry

            lax.fori_loop(0, tiles, key_tile, 0)

        @pl.when(jnp.logical_not(block_needed))
        def _(span=span):
            kept[:, span] = jnp.zeros((size, rows), kept.dtype)
            sent[:, span] = jnp.zeros((size, rows), sent.dtype)


def finish_kernel(heads, scale, dq, out):
    rows, size = out.shape[0], dq.shape[0]
    for t in range(rows // TILE):
        for h in range(heads):
            span = slice((t * heads + h) * TILE, (t * heads + h + 1) * TILE)
            out[t * TILE : (t + 1) * TILE, h * size : (h + 1) * size] = (
                (dq[:, span] * scale).T.astype(out.dtype)
            )


def finish_call(dq, heads):
    size, rows = dq.shape[0], dq.shape[1] // heads
    vmem = pl.BlockSpec(memory_space=pltpu.VMEM)
    return pl.pallas_call(
        functools.partial(finish_kernel, heads, size ** (-0.5)),
        out_shape=jax.ShapeDtypeStruct((rows, heads * size), jnp.bfloat16),
        in_specs=[vmem],
        out_specs=vmem,
        cost_estimate=pl.CostEstimate(flops=2**31, bytes_accessed=2**20, transcendentals=0),
    )(dq)


def block_call(distances, first, heads, place, docs, q, g, a, b, mine, other):
    if first:
        rows, width = q.shape
    else:
        rows, width = q.shape[1] // heads, q.shape[0] * heads
    size = width // heads
    blocks = len(distances)
    total = blocks * rows
    scale = size ** (-0.5)
    smem = pl.BlockSpec(memory_space=pltpu.SMEM)
    vmem = pl.BlockSpec(memory_space=pltpu.VMEM)
    operands = [q, g, a, b] + mine + other
    outs = [
        jax.ShapeDtypeStruct((size, heads * rows), jnp.float32)
    ]
    if first:
        outs.append(jax.ShapeDtypeStruct((8, heads * rows), jnp.float32))
        outs += [jax.ShapeDtypeStruct((size, heads * rows), jnp.bfloat16)] * 2
    outs += [
        jax.ShapeDtypeStruct((size, total), jnp.float32),
        jax.ShapeDtypeStruct((size, total), jnp.bfloat16),
    ]
    scratch = [
        pltpu.VMEM((rows, size), jnp.bfloat16),
        pltpu.VMEM((size, rows), jnp.bfloat16),
        pltpu.VMEM((rows, size), jnp.bfloat16),
        pltpu.VMEM((size, TILE), jnp.float32),
        pltpu.VMEM((size, TILE), jnp.float32),
    ]
    specs = [smem, smem] + [vmem] * len(operands)
    if first:
        hbm = pl.BlockSpec(memory_space=pltpu.HBM)
        specs = [smem, smem, hbm, hbm, vmem, hbm] + [vmem] * len(mine + other)
        scratch += [pltpu.VMEM((rows, width), jnp.bfloat16)] * 3
        scratch.append(pltpu.SemaphoreType.DMA((3,)))
    return pl.pallas_call(
        functools.partial(block_kernel, distances, first, heads, scale),
        out_shape=outs,
        in_specs=specs,
        out_specs=[vmem] * len(outs),
        scratch_shapes=scratch,
        input_output_aliases={} if first else {5: 0},
        cost_estimate=pl.CostEstimate(
            flops=blocks * 10 * rows * rows * width * 2,
            bytes_accessed=4 * rows * width,
            transcendentals=blocks * heads * rows * rows,
        ),
        compiler_params=pltpu.CompilerParams(vmem_limit_bytes=32 * 1024 * 1024),
    )(place, docs, *operands)


def local(queries, key_states, value_states, attn_out, grad_out, log_norm, doc_lengths):
    rows, half = key_states.shape
    heads = log_norm.shape[0]
    scale = (2 * half) ** (-0.5)
    ctx_index = lax.axis_index("ctx")
    place = jnp.stack([ctx_index, lax.axis_index("head") % 2]).astype(jnp.int32)
    own = jnp.concatenate([key_states.T, value_states.T], axis=0)
    own_other = partner(own)
    arrived = {}
    for d in (4, 3, 2, 1):
        arrived[d] = passed_along(own, d, 0 if RELAY and d == 3 else None)
    if RELAY:
        arrived[3] = jnp.where(ctx_index % 2 == 1, arrived[3], neighbour(arrived[4]))

    def stage(distances, blocks, others, first=False):
        return block_call(
            distances, first, heads, place, doc_lengths, q, g, facts, dq, blocks, others
        )

    def returns(distances, kept, sent):
        terms = (kept + partner(sent).astype(jnp.float32)).astype(jnp.bfloat16)
        return terms, [
            passed_along(terms[:, j * rows : (j + 1) * rows], -d)
            for j, d in enumerate(distances)
        ]

    q, g, facts, dq = queries, grad_out, log_norm, attn_out
    dq, facts, q, g, own_kept, own_sent = stage((0,), [own], [own_other], True)
    arrived, dq, own_sent = lax.optimization_barrier((arrived, dq, own_sent))
    others = {d: partner(a) for d, a in arrived.items()}
    total = own_kept + partner(own_sent).astype(jnp.float32)
    received = []
    for number, distances in enumerate(STAGES):
        if number and TIE:
            dq, terms = lax.optimization_barrier((dq, terms))
        dq, kept, sent = stage(
            distances, [arrived[d] for d in distances], [others[d] for d in distances]
        )
        if number and TIE:
            sent, received = lax.optimization_barrier((sent, received))
        terms, backs = returns(distances, kept, sent)
        received = received + backs
    for back in received:
        total = total + back.astype(jnp.float32)
    grad_keys = (total[:half] * scale).astype(jnp.bfloat16).T
    grad_values = total[half:].astype(jnp.bfloat16).T
    return finish_call(dq, heads), grad_keys, grad_values


def solution(mesh):
    in_specs = (
        P("ctx", "head"),
        P("ctx", "head"),
        P("ctx", "head"),
        P("ctx", "head"),
        P("ctx", "head"),
        P("head", "ctx"),
        P(),
    )
    out_specs = (P("ctx", "head"), P("ctx", "head"), P("ctx", "head"))
    return jax.shard_map(local, mesh=mesh, in_specs=in_specs, out_specs=out_specs, check_vma=False)
```

```python
import functools

import jax
import jax.numpy as jnp
from jax import lax
from jax.experimental import pallas as pl
from jax.experimental.pallas import tpu as pltpu
from jax.sharding import PartitionSpec as P

STAGES = ((4, 3), (2, 1))
FORWARD = (4, 3, 2, 1)
TIE = 1
TILE = 256
LOG2E = 1.4426950408889634
NN = (((1,), (0,)), ((), ()))
NT = (((1,), (1,)), ((), ()))


def partner(value):
    count = lax.axis_size("head")
    return lax.ppermute(value, "head", [(i, i ^ 1) for i in range(count)])


def passed_along(value, by):
    count = lax.axis_size("ctx")
    return lax.ppermute(value, "ctx", [(i, (i + by) % count) for i in range(count)])


def exchanged(value, by):
    count = lax.axis_size("ctx")
    pairs = [(i, (i + by) % count) for i in range(0, count, 2)]
    return lax.ppermute(value, "ctx", pairs + [(j, i) for i, j in pairs])


def neighbour(value):
    count = lax.axis_size("ctx")
    return lax.ppermute(value, "ctx", [(i, i ^ 1) for i in range(count)])


def dot(a, b, dims=NN):
    return lax.dot_general(a, b, dims, preferred_element_type=jnp.float32)


def row_start(docs, position):
    def step(j, state):
        total, found = state
        total = total + docs[j]
        return total, jnp.where(total <= position, total, found)

    zero = jnp.int32(0)
    return lax.fori_loop(0, docs.shape[0], step, (zero, zero), unroll=True)[1]


def row_starts(docs, positions):
    def step(j, state):
        total, found = state
        total = total + docs[j]
        return total, jnp.where(positions >= total, total, found)

    start = (jnp.int32(0), jnp.zeros_like(positions))
    return lax.fori_loop(0, docs.shape[0], step, start, unroll=True)[1]


def prepare_rows(first_pos, docs, g, norms, attn_out, facts, tiles, heads, size):
    rows = tiles * TILE
    positions = first_pos + lax.broadcasted_iota(jnp.int32, (1, rows), 1)
    starts = row_starts(docs, positions).astype(jnp.float32)
    positions = positions.astype(jnp.float32)
    ones = jnp.ones((8, size), jnp.bfloat16)
    for h in range(heads):
        cols = slice(h * size, (h + 1) * size)
        product = attn_out[:, cols].astype(jnp.float32) * g[:, cols].astype(jnp.float32)
        high = product.astype(jnp.bfloat16)
        low = (product - high.astype(jnp.float32)).astype(jnp.bfloat16)
        delta = (dot(ones, high, NT) + dot(ones, low, NT))[:1, :]
        level = norms[h : h + 1, :] * LOG2E
        for t in range(tiles):
            span = slice((t * heads + h) * TILE, (t * heads + h + 1) * TILE)
            part = slice(t * TILE, (t + 1) * TILE)
            facts[0:1, span] = level[:, part]
            facts[1:2, span] = delta[:, part]
            facts[2:3, span] = starts[:, part]
            facts[3:4, span] = positions[:, part]


def block_kernel(distances, first, heads, scale, place, docs, qt, gt, *rest):
    blocks = len(distances)
    rest = list(rest)
    if first:
        norms, attn_hbm = rest.pop(0), rest.pop(0)
    else:
        facts, prior = rest.pop(0), rest.pop(0)
    mine, other, rest = rest[:blocks], rest[blocks : 2 * blocks], rest[2 * blocks :]
    query_out = rest.pop(0)
    if first:
        facts = rest.pop(0)
        q_hbm, g_hbm, qt, gt = qt, gt, rest.pop(0), rest.pop(0)
    kept, sent, keys, keys_t, values, dk, dv = rest[:7]
    dq = query_out
    if first:
        attn_out, q, g, sems = rest[7:]
        pairs = ((attn_hbm, attn_out), (g_hbm, g), (q_hbm, q))
        loads = [pltpu.make_async_copy(a, b, sems.at[i]) for i, (a, b) in enumerate(pairs)]
        for load in loads:
            load.start()
    size, rows = qt.shape[0], qt.shape[1] // heads
    half = size // 2
    tiles = rows // TILE
    wide = heads * TILE
    ctx_index, upper = place[0], place[1] == 1
    first_pos = ctx_index * rows
    lowest = [row_start(docs, first_pos + t * TILE) for t in range(tiles)]
    highest = [row_start(docs, first_pos + (t + 1) * TILE - 1) for t in range(tiles)]

    if first:
        for load in loads:
            load.wait()
        prepare_rows(first_pos, docs, g, norms, attn_out, facts, tiles, heads, size)
        for t in range(tiles):
            for h in range(heads):
                span = slice((t * heads + h) * TILE, (t * heads + h + 1) * TILE)
                part = slice(t * TILE, (t + 1) * TILE)
                cols = slice(h * size, (h + 1) * size)
                qt[:, span] = q[part, cols].T
                gt[:, span] = g[part, cols].T
        dq[...] = jnp.zeros_like(dq)

    for j, distance in enumerate(distances):
        block_lo = (ctx_index - distance) * rows
        block_needed = (ctx_index >= distance) & (block_lo + rows > lowest[0])
        span = slice(j * rows, (j + 1) * rows)

        @pl.when(block_needed)
        def _(j=j, span=span, block_lo=block_lo):
            a, b = mine[j][...], other[j][...]
            lower = jnp.where(upper, b, a)
            above = jnp.where(upper, a, b)
            key_rows = jnp.concatenate([lower[:half, :], above[:half, :]], axis=0)
            value_rows = jnp.concatenate([lower[half:, :], above[half:, :]], axis=0)
            keys_t[...] = key_rows
            keys[...] = key_rows.T
            values[...] = value_rows.T

            def key_tile(index, carry):
                base = pl.multiple_of(index * TILE, TILE)
                key_lo = block_lo + base
                dk[...] = jnp.zeros_like(dk)
                dv[...] = jnp.zeros_like(dv)

                def query_tile(t, inner):
                    query_lo = first_pos + t * TILE
                    least, top = lowest[0], highest[0]
                    for other_t in range(1, tiles):
                        least = jnp.where(t == other_t, lowest[other_t], least)
                        top = jnp.where(t == other_t, highest[other_t], top)
                    needed = (key_lo <= query_lo + TILE - 1) & (key_lo + TILE - 1 >= least)

                    inside = (key_lo + TILE - 1 <= query_lo) & (key_lo >= top)

                    def tile(masked):
                        k = keys[pl.ds(base, TILE), :]
                        v = values[pl.ds(base, TILE), :]
                        kt = keys_t[:, pl.ds(base, TILE)]
                        lanes = pl.ds(pl.multiple_of(t * wide, wide), wide)
                        qs, gs = qt[:, lanes], gt[:, lanes]
                        scores = dot(k, qs) * (scale * LOG2E)
                        probs = jnp.exp2(scores - facts[0:1, lanes])
                        if masked:
                            offset = lax.broadcasted_iota(jnp.int32, (TILE, wide), 0)
                            offset = offset.astype(jnp.float32)
                            shift = key_lo.astype(jnp.float32)
                            allowed = (offset <= facts[3:4, lanes] - shift) & (
                                offset >= facts[2:3, lanes] - shift
                            )
                            probs = jnp.where(allowed, probs, 0.0)
                        dscores = probs * (dot(v, gs) - facts[1:2, lanes])
                        probs = probs.astype(jnp.bfloat16)
                        dscores = dscores.astype(jnp.bfloat16)
                        dv[...] += dot(gs, probs, NT)
                        dk[...] += dot(qs, dscores, NT)
                        dq[:, lanes] += dot(kt, dscores)

                    pl.when(inside)(functools.partial(tile, False))
                    pl.when(needed & jnp.logical_not(inside))(functools.partial(tile, True))

                    return inner

                lax.fori_loop(0, tiles, query_tile, 0)
                key_sum, value_sum = dk[...], dv[...]
                lower = jnp.concatenate([key_sum[:half], value_sum[:half]], axis=0)
                above = jnp.concatenate([key_sum[half:], value_sum[half:]], axis=0)
                out = pl.ds(pl.multiple_of(j * rows + base, TILE), TILE)
                kept[:, out] = jnp.where(upper, above, lower)
                sent[:, out] = jnp.where(upper, lower, above).astype(sent.dtype)
                return carry

            lax.fori_loop(0, tiles, key_tile, 0)

        @pl.when(jnp.logical_not(block_needed))
        def _(span=span):
            kept[:, span] = jnp.zeros((size, rows), kept.dtype)
            sent[:, span] = jnp.zeros((size, rows), sent.dtype)


def finish_kernel(heads, scale, dq, out):
    rows, size = out.shape[0], dq.shape[0]
    for t in range(rows // TILE):
        for h in range(heads):
            span = slice((t * heads + h) * TILE, (t * heads + h + 1) * TILE)
            out[t * TILE : (t + 1) * TILE, h * size : (h + 1) * size] = (
                (dq[:, span] * scale).astype(out.dtype).T
            )


def finish_call(dq, heads):
    size, rows = dq.shape[0], dq.shape[1] // heads
    vmem = pl.BlockSpec(memory_space=pltpu.VMEM)
    return pl.pallas_call(
        functools.partial(finish_kernel, heads, size ** (-0.5)),
        out_shape=jax.ShapeDtypeStruct((rows, heads * size), jnp.bfloat16),
        in_specs=[vmem],
        out_specs=vmem,
        cost_estimate=pl.CostEstimate(flops=2**31, bytes_accessed=2**20, transcendentals=0),
    )(dq)


def block_call(distances, first, heads, place, docs, q, g, a, b, mine, other):
    if first:
        rows, width = q.shape
    else:
        rows, width = q.shape[1] // heads, q.shape[0] * heads
    size = width // heads
    blocks = len(distances)
    total = blocks * rows
    scale = size ** (-0.5)
    smem = pl.BlockSpec(memory_space=pltpu.SMEM)
    vmem = pl.BlockSpec(memory_space=pltpu.VMEM)
    operands = [q, g, a, b] + mine + other
    outs = [
        jax.ShapeDtypeStruct((size, heads * rows), jnp.float32)
    ]
    if first:
        outs.append(jax.ShapeDtypeStruct((8, heads * rows), jnp.float32))
        outs += [jax.ShapeDtypeStruct((size, heads * rows), jnp.bfloat16)] * 2
    outs += [
        jax.ShapeDtypeStruct((size, total), jnp.float32),
        jax.ShapeDtypeStruct((size, total), jnp.bfloat16),
    ]
    scratch = [
        pltpu.VMEM((rows, size), jnp.bfloat16),
        pltpu.VMEM((size, rows), jnp.bfloat16),
        pltpu.VMEM((rows, size), jnp.bfloat16),
        pltpu.VMEM((size, TILE), jnp.float32),
        pltpu.VMEM((size, TILE), jnp.float32),
    ]
    specs = [smem, smem] + [vmem] * len(operands)
    if first:
        hbm = pl.BlockSpec(memory_space=pltpu.HBM)
        specs = [smem, smem, hbm, hbm, vmem, hbm] + [vmem] * len(mine + other)
        scratch += [pltpu.VMEM((rows, width), jnp.bfloat16)] * 3
        scratch.append(pltpu.SemaphoreType.DMA((3,)))
    return pl.pallas_call(
        functools.partial(block_kernel, distances, first, heads, scale),
        out_shape=outs,
        in_specs=specs,
        out_specs=[vmem] * len(outs),
        scratch_shapes=scratch,
        input_output_aliases={} if first else {5: 0},
        cost_estimate=pl.CostEstimate(
            flops=blocks * 10 * rows * rows * width * 2,
            bytes_accessed=4 * rows * width,
            transcendentals=blocks * heads * rows * rows,
        ),
        compiler_params=pltpu.CompilerParams(vmem_limit_bytes=32 * 1024 * 1024),
    )(place, docs, *operands)


def local(queries, key_states, value_states, attn_out, grad_out, log_norm, doc_lengths):
    rows, half = key_states.shape
    heads = log_norm.shape[0]
    scale = (2 * half) ** (-0.5)
    ctx_index = lax.axis_index("ctx")
    place = jnp.stack([ctx_index, lax.axis_index("head") % 2]).astype(jnp.int32)
    own = jnp.concatenate([key_states.T, value_states.T], axis=0)
    own_other = partner(own)
    arrived = {}
    for d in FORWARD:
        arrived[d] = (exchanged if d == 3 else passed_along)(own, d)
    odd = ctx_index % 2 == 1

    def stage(distances, blocks, others, first=False):
        return block_call(
            distances, first, heads, place, doc_lengths, q, g, facts, dq, blocks, others
        )

    in_hbm = lambda x: pltpu.with_memory_space_constraint(x, pltpu.HBM)
    q, g, facts, dq = in_hbm(queries), in_hbm(grad_out), log_norm, in_hbm(attn_out)
    dq, facts, q, g, own_kept, own_sent = stage((0,), [own], [own_other], True)
    arrived[3] = jnp.where(odd, arrived[3], neighbour(arrived[4]))
    arrived, dq, own_sent = lax.optimization_barrier((arrived, dq, own_sent))
    others = {d: partner(a) for d, a in arrived.items()}
    total = own_kept + partner(own_sent).astype(jnp.float32)
    far, near = STAGES
    dq, kept, sent = stage(far, [arrived[d] for d in far], [others[d] for d in far])
    terms = (kept + partner(sent).astype(jnp.float32)).astype(jnp.bfloat16)
    dq, terms = lax.optimization_barrier((dq, terms))
    relayed = passed_along(terms, -2)
    dq, kept, sent = stage(near, [arrived[d] for d in near], [others[d] for d in near])
    if TIE:
        sent, relayed = lax.optimization_barrier((sent, relayed))
    terms = kept + partner(sent).astype(jnp.float32) + relayed.astype(jnp.float32)
    terms = terms.astype(jnp.bfloat16)
    for j, d in enumerate(near):
        back = passed_along(terms[:, j * rows : (j + 1) * rows], -d)
        total = total + back.astype(jnp.float32)
    grad_keys = (total[:half] * scale).astype(jnp.bfloat16).T
    grad_values = total[half:].astype(jnp.bfloat16).T
    return finish_call(dq, heads), grad_keys, grad_values


def solution(mesh):
    in_specs = (
        P("ctx", "head"),
        P("ctx", "head"),
        P("ctx", "head"),
        P("ctx", "head"),
        P("ctx", "head"),
        P("head", "ctx"),
        P(),
    )
    out_specs = (P("ctx", "head"), P("ctx", "head"), P("ctx", "head"))
    return jax.shard_map(local, mesh=mesh, in_specs=in_specs, out_specs=out_specs, check_vma=False)
```

```python
import functools

import jax
import jax.numpy as jnp
from jax import lax
from jax.experimental import pallas as pl
from jax.experimental.pallas import tpu as pltpu
from jax.sharding import PartitionSpec as P

DIRECT = False
TILE = 256
LOG2E = 1.4426950408889634
NN = (((1,), (0,)), ((), ()))
NT = (((1,), (1,)), ((), ()))


def partner(value):
    count = lax.axis_size("head")
    return lax.ppermute(value, "head", [(i, i ^ 1) for i in range(count)])


def passed_along(value, by):
    count = lax.axis_size("ctx")
    return lax.ppermute(value, "ctx", [(i, (i + by) % count) for i in range(count)])


def dot(a, b, dims=NN):
    return lax.dot_general(a, b, dims, preferred_element_type=jnp.float32)


def row_start(docs, position):
    def step(j, state):
        total, found = state
        total = total + docs[j]
        return total, jnp.where(total <= position, total, found)

    zero = jnp.int32(0)
    return lax.fori_loop(0, docs.shape[0], step, (zero, zero), unroll=True)[1]


def row_starts(docs, positions):
    def step(j, state):
        total, found = state
        total = total + docs[j]
        return total, jnp.where(positions >= total, total, found)

    start = (jnp.int32(0), jnp.zeros_like(positions))
    return lax.fori_loop(0, docs.shape[0], step, start, unroll=True)[1]


def prepare_rows(first_pos, docs, g, norms, attn_out, facts, tiles, heads, size):
    rows = tiles * TILE
    positions = first_pos + lax.broadcasted_iota(jnp.int32, (1, rows), 1)
    starts = row_starts(docs, positions).astype(jnp.float32)
    positions = positions.astype(jnp.float32)
    ones = jnp.ones((8, size), jnp.bfloat16)
    for h in range(heads):
        cols = slice(h * size, (h + 1) * size)
        product = attn_out[:, cols].astype(jnp.float32) * g[:, cols].astype(jnp.float32)
        high = product.astype(jnp.bfloat16)
        low = (product - high.astype(jnp.float32)).astype(jnp.bfloat16)
        delta = (dot(ones, high, NT) + dot(ones, low, NT))[:1, :]
        level = norms[h : h + 1, :] * LOG2E
        for t in range(tiles):
            span = slice((t * heads + h) * TILE, (t * heads + h + 1) * TILE)
            part = slice(t * TILE, (t + 1) * TILE)
            facts[0:1, span] = level[:, part]
            facts[1:2, span] = delta[:, part]
            facts[2:3, span] = starts[:, part]
            facts[3:4, span] = positions[:, part]


def block_kernel(distances, first, heads, scale, place, docs, qt, gt, *rest):
    blocks = len(distances)
    rest = list(rest)
    if first:
        norms, attn_hbm = rest.pop(0), rest.pop(0)
    else:
        facts, prior = rest.pop(0), rest.pop(0)
    mine, other, rest = rest[0], rest[1], rest[2:]
    query_out = rest.pop(0)
    if first:
        facts = rest.pop(0)
        q_hbm, g_hbm, qt, gt = qt, gt, rest.pop(0), rest.pop(0)
    kept, sent, keys, keys_t, values, dk, dv = rest[:7]
    dq = query_out
    if first:
        attn_out, q, g, sems = rest[7:]
        pairs = ((attn_hbm, attn_out), (g_hbm, g), (q_hbm, q))
        loads = [pltpu.make_async_copy(a, b, sems.at[i]) for i, (a, b) in enumerate(pairs)]
        for load in loads:
            load.start()
    size, rows = qt.shape[0], qt.shape[1] // heads
    half = size // 2
    tiles = rows // TILE
    wide = heads * TILE
    ctx_index, upper = place[0], place[1] == 1
    first_pos = ctx_index * rows
    lowest = [row_start(docs, first_pos + t * TILE) for t in range(tiles)]
    highest = [row_start(docs, first_pos + (t + 1) * TILE - 1) for t in range(tiles)]

    if first:
        for load in loads:
            load.wait()
        prepare_rows(first_pos, docs, g, norms, attn_out, facts, tiles, heads, size)
        for t in range(tiles):
            for h in range(heads):
                span = slice((t * heads + h) * TILE, (t * heads + h + 1) * TILE)
                part = slice(t * TILE, (t + 1) * TILE)
                cols = slice(h * size, (h + 1) * size)
                qt[:, span] = q[part, cols].T
                gt[:, span] = g[part, cols].T
        dq[...] = jnp.zeros_like(dq)

    for j, distance in enumerate(distances):
        block_lo = (ctx_index - distance) * rows
        block_needed = (ctx_index >= distance) & (block_lo + rows > lowest[0])
        span = slice(j * rows, (j + 1) * rows)

        @pl.when(block_needed)
        def _(j=j, span=span, block_lo=block_lo):
            a, b = mine[:, span], other[:, span]
            lower = jnp.where(upper, b, a)
            above = jnp.where(upper, a, b)
            key_rows = jnp.concatenate([lower[:half, :], above[:half, :]], axis=0)
            value_rows = jnp.concatenate([lower[half:, :], above[half:, :]], axis=0)
            keys_t[...] = key_rows
            keys[...] = key_rows.T
            values[...] = value_rows.T

            def key_tile(index, carry):
                base = pl.multiple_of(index * TILE, TILE)
                key_lo = block_lo + base
                dk[...] = jnp.zeros_like(dk)
                dv[...] = jnp.zeros_like(dv)

                def query_tile(t, inner):
                    query_lo = first_pos + t * TILE
                    least, top = lowest[0], highest[0]
                    for other_t in range(1, tiles):
                        least = jnp.where(t == other_t, lowest[other_t], least)
                        top = jnp.where(t == other_t, highest[other_t], top)
                    needed = (key_lo <= query_lo + TILE - 1) & (key_lo + TILE - 1 >= least)

                    inside = (key_lo + TILE - 1 <= query_lo) & (key_lo >= top)

                    def tile(masked):
                        k = keys[pl.ds(base, TILE), :]
                        v = values[pl.ds(base, TILE), :]
                        kt = keys_t[:, pl.ds(base, TILE)]
                        lanes = pl.ds(pl.multiple_of(t * wide, wide), wide)
                        qs, gs = qt[:, lanes], gt[:, lanes]
                        scores = dot(k, qs) * (scale * LOG2E)
                        probs = jnp.exp2(scores - facts[0:1, lanes])
                        if masked:
                            offset = lax.broadcasted_iota(jnp.int32, (TILE, wide), 0)
                            offset = offset.astype(jnp.float32)
                            shift = key_lo.astype(jnp.float32)
                            allowed = (offset <= facts[3:4, lanes] - shift) & (
                                offset >= facts[2:3, lanes] - shift
                            )
                            probs = jnp.where(allowed, probs, 0.0)
                        dscores = probs * (dot(v, gs) - facts[1:2, lanes])
                        probs = probs.astype(jnp.bfloat16)
                        dscores = dscores.astype(jnp.bfloat16)
                        dv[...] += dot(gs, probs, NT)
                        dk[...] += dot(qs, dscores, NT)
                        dq[:, lanes] += dot(kt, dscores)

                    pl.when(inside)(functools.partial(tile, False))
                    pl.when(needed & jnp.logical_not(inside))(functools.partial(tile, True))

                    return inner

                lax.fori_loop(0, tiles, query_tile, 0)
                key_sum, value_sum = dk[...], dv[...]
                lower = jnp.concatenate([key_sum[:half], value_sum[:half]], axis=0)
                above = jnp.concatenate([key_sum[half:], value_sum[half:]], axis=0)
                out = pl.ds(pl.multiple_of(j * rows + base, TILE), TILE)
                kept[:, out] = jnp.where(upper, above, lower)
                sent[:, out] = jnp.where(upper, lower, above).astype(sent.dtype)
                return carry

            lax.fori_loop(0, tiles, key_tile, 0)

        @pl.when(jnp.logical_not(block_needed))
        def _(span=span):
            kept[:, span] = jnp.zeros((size, rows), kept.dtype)
            sent[:, span] = jnp.zeros((size, rows), sent.dtype)


def finish_kernel(heads, scale, dq, out):
    rows, size = out.shape[0], dq.shape[0]
    for t in range(rows // TILE):
        for h in range(heads):
            span = slice((t * heads + h) * TILE, (t * heads + h + 1) * TILE)
            out[t * TILE : (t + 1) * TILE, h * size : (h + 1) * size] = (
                (dq[:, span] * scale).astype(out.dtype).T
            )


def finish_call(dq, heads):
    size, rows = dq.shape[0], dq.shape[1] // heads
    vmem = pl.BlockSpec(memory_space=pltpu.VMEM)
    return pl.pallas_call(
        functools.partial(finish_kernel, heads, size ** (-0.5)),
        out_shape=jax.ShapeDtypeStruct((rows, heads * size), jnp.bfloat16),
        in_specs=[vmem],
        out_specs=vmem,
        cost_estimate=pl.CostEstimate(flops=2**31, bytes_accessed=2**20, transcendentals=0),
    )(dq)


def block_call(distances, first, heads, place, docs, q, g, a, b, mine, other):
    if first:
        rows, width = q.shape
    else:
        rows, width = q.shape[1] // heads, q.shape[0] * heads
    size = width // heads
    blocks = len(distances)
    total = blocks * rows
    scale = size ** (-0.5)
    smem = pl.BlockSpec(memory_space=pltpu.SMEM)
    vmem = pl.BlockSpec(memory_space=pltpu.VMEM)
    operands = [q, g, a, b, mine, other]
    outs = [
        jax.ShapeDtypeStruct((size, heads * rows), jnp.float32)
    ]
    if first:
        outs.append(jax.ShapeDtypeStruct((8, heads * rows), jnp.float32))
        outs += [jax.ShapeDtypeStruct((size, heads * rows), jnp.bfloat16)] * 2
    outs += [
        jax.ShapeDtypeStruct((size, total), jnp.float32),
        jax.ShapeDtypeStruct((size, total), jnp.bfloat16),
    ]
    scratch = [
        pltpu.VMEM((rows, size), jnp.bfloat16),
        pltpu.VMEM((size, rows), jnp.bfloat16),
        pltpu.VMEM((rows, size), jnp.bfloat16),
        pltpu.VMEM((size, TILE), jnp.float32),
        pltpu.VMEM((size, TILE), jnp.float32),
    ]
    specs = [smem, smem] + [vmem] * len(operands)
    if first:
        hbm = pl.BlockSpec(memory_space=pltpu.HBM)
        specs = [smem, smem, hbm, hbm, vmem, hbm, vmem, vmem]
        scratch += [pltpu.VMEM((rows, width), jnp.bfloat16)] * 3
        scratch.append(pltpu.SemaphoreType.DMA((3,)))
    return pl.pallas_call(
        functools.partial(block_kernel, distances, first, heads, scale),
        out_shape=outs,
        in_specs=specs,
        out_specs=[vmem] * len(outs),
        scratch_shapes=scratch,
        input_output_aliases={} if first else {5: 0},
        cost_estimate=pl.CostEstimate(
            flops=blocks * 10 * rows * rows * width * 2,
            bytes_accessed=4 * rows * width,
            transcendentals=blocks * heads * rows * rows,
        ),
        compiler_params=pltpu.CompilerParams(vmem_limit_bytes=32 * 1024 * 1024),
    )(place, docs, *operands)


def local(queries, key_states, value_states, attn_out, grad_out, log_norm, doc_lengths):
    rows, half = key_states.shape
    heads = log_norm.shape[0]
    scale = (2 * half) ** (-0.5)
    place = jnp.stack([lax.axis_index("ctx"), lax.axis_index("head") % 2]).astype(jnp.int32)
    own = jnp.concatenate([key_states.T, value_states.T], axis=0)
    own_other = partner(own)
    second, first = passed_along(own, 2), passed_along(own, 1)

    def stage(distances, blocks, others, first=False):
        return block_call(
            distances, first, heads, place, doc_lengths, q, g, facts, dq, blocks, others
        )

    def pair_sum(kept, sent):
        return kept + partner(sent).astype(jnp.float32)

    in_hbm = lambda x: pltpu.with_memory_space_constraint(x, pltpu.HBM)
    q, g, facts, dq = in_hbm(queries), in_hbm(grad_out), log_norm, in_hbm(attn_out)
    dq, facts, q, g, own_kept, own_sent = stage((0,), own, own_other, True)
    second, first, dq = lax.optimization_barrier((second, first, dq))
    near = jnp.concatenate([second, first], axis=1)
    far = passed_along(near, 2)
    total = pair_sum(own_kept, own_sent)
    dq, near_kept, near_sent = stage((2, 1), near, partner(near))
    far, near_sent, dq = lax.optimization_barrier((far, near_sent, dq))
    near_sum = pair_sum(near_kept, near_sent)
    if DIRECT:
        near_terms = near_sum.astype(jnp.bfloat16)
        dq, near_terms = lax.optimization_barrier((dq, near_terms))
        backs = [passed_along(near_terms[:, :rows], -2), passed_along(near_terms[:, rows:], -1)]
        dq, far_kept, far_sent = stage((4, 3), far, partner(far))
        far_sent, backs = lax.optimization_barrier((far_sent, backs))
        far_terms = pair_sum(far_kept, far_sent).astype(jnp.bfloat16)
        backs += [passed_along(far_terms[:, :rows], -4), passed_along(far_terms[:, rows:], -3)]
    else:
        dq, far_kept, far_sent = stage((4, 3), far, partner(far))
        far_terms = pair_sum(far_kept, far_sent).astype(jnp.bfloat16)
        near_sum = near_sum + passed_along(far_terms, -2).astype(jnp.float32)
        near_terms = near_sum.astype(jnp.bfloat16)
        backs = [passed_along(near_terms[:, :rows], -2), passed_along(near_terms[:, rows:], -1)]
    for back in backs:
        total = total + back.astype(jnp.float32)
    grad_keys = (total[:half] * scale).astype(jnp.bfloat16).T
    grad_values = total[half:].astype(jnp.bfloat16).T
    return finish_call(dq, heads), grad_keys, grad_values


def solution(mesh):
    in_specs = (
        P("ctx", "head"),
        P("ctx", "head"),
        P("ctx", "head"),
        P("ctx", "head"),
        P("ctx", "head"),
        P("head", "ctx"),
        P(),
    )
    out_specs = (P("ctx", "head"), P("ctx", "head"), P("ctx", "head"))
    return jax.shard_map(local, mesh=mesh, in_specs=in_specs, out_specs=out_specs, check_vma=False)
```

```python
import functools

import jax
import jax.numpy as jnp
from jax import lax
from jax.experimental import pallas as pl
from jax.experimental.pallas import tpu as pltpu
from jax.sharding import PartitionSpec as P

DIRECT = False
TILE = 256
LOG2E = 1.4426950408889634
NN = (((1,), (0,)), ((), ()))
NT = (((1,), (1,)), ((), ()))


def partner(value):
    count = lax.axis_size("head")
    return lax.ppermute(value, "head", [(i, i ^ 1) for i in range(count)])


def passed_along(value, by):
    count = lax.axis_size("ctx")
    return lax.ppermute(value, "ctx", [(i, (i + by) % count) for i in range(count)])


def dot(a, b, dims=NN):
    return lax.dot_general(a, b, dims, preferred_element_type=jnp.float32)


def row_start(docs, position):
    def step(j, state):
        total, found = state
        total = total + docs[j]
        return total, jnp.where(total <= position, total, found)

    zero = jnp.int32(0)
    return lax.fori_loop(0, docs.shape[0], step, (zero, zero), unroll=True)[1]


def row_starts(docs, positions):
    def step(j, state):
        total, found = state
        total = total + docs[j]
        return total, jnp.where(positions >= total, total, found)

    start = (jnp.int32(0), jnp.zeros_like(positions))
    return lax.fori_loop(0, docs.shape[0], step, start, unroll=True)[1]


def prepare_rows(first_pos, docs, g, norms, attn_out, facts, tiles, heads, size):
    rows = tiles * TILE
    positions = first_pos + lax.broadcasted_iota(jnp.int32, (1, rows), 1)
    starts = row_starts(docs, positions).astype(jnp.float32)
    positions = positions.astype(jnp.float32)
    ones = jnp.ones((8, size), jnp.bfloat16)
    for h in range(heads):
        cols = slice(h * size, (h + 1) * size)
        product = attn_out[:, cols].astype(jnp.float32) * g[:, cols].astype(jnp.float32)
        high = product.astype(jnp.bfloat16)
        low = (product - high.astype(jnp.float32)).astype(jnp.bfloat16)
        delta = (dot(ones, high, NT) + dot(ones, low, NT))[:1, :]
        level = norms[h : h + 1, :] * LOG2E
        for t in range(tiles):
            span = slice((t * heads + h) * TILE, (t * heads + h + 1) * TILE)
            part = slice(t * TILE, (t + 1) * TILE)
            facts[0:1, span] = level[:, part]
            facts[1:2, span] = delta[:, part]
            facts[2:3, span] = starts[:, part]
            facts[3:4, span] = positions[:, part]


def block_kernel(distances, first, heads, scale, place, docs, qt, gt, *rest):
    blocks = len(distances)
    rest = list(rest)
    if first:
        norms, attn_hbm = rest.pop(0), rest.pop(0)
    else:
        facts, prior = rest.pop(0), rest.pop(0)
    mine, other, rest = rest[0], rest[1], rest[2:]
    query_out = rest.pop(0)
    if first:
        facts = rest.pop(0)
        q_hbm, g_hbm, qt, gt = qt, gt, rest.pop(0), rest.pop(0)
    kept, sent, keys, keys_t, values, dk, dv = rest[:7]
    dq = query_out
    if first:
        attn_out, q, g, sems = rest[7:]
        pairs = ((attn_hbm, attn_out), (g_hbm, g), (q_hbm, q))
        loads = [pltpu.make_async_copy(a, b, sems.at[i]) for i, (a, b) in enumerate(pairs)]
        for load in loads:
            load.start()
    size, rows = qt.shape[0], qt.shape[1] // heads
    half = size // 2
    tiles = rows // TILE
    wide = heads * TILE
    ctx_index, upper = place[0], place[1] == 1
    first_pos = ctx_index * rows
    lowest = [row_start(docs, first_pos + t * TILE) for t in range(tiles)]
    highest = [row_start(docs, first_pos + (t + 1) * TILE - 1) for t in range(tiles)]

    if first:
        for load in loads:
            load.wait()
        prepare_rows(first_pos, docs, g, norms, attn_out, facts, tiles, heads, size)
        for t in range(tiles):
            for h in range(heads):
                span = slice((t * heads + h) * TILE, (t * heads + h + 1) * TILE)
                part = slice(t * TILE, (t + 1) * TILE)
                cols = slice(h * size, (h + 1) * size)
                qt[:, span] = q[part, cols].T
                gt[:, span] = g[part, cols].T
        dq[...] = jnp.zeros_like(dq)

    def block(j, state):
        block_lo = (ctx_index - distances[0] + j) * rows
        block_needed = (block_lo >= 0) & (block_lo + rows > lowest[0])
        span = pl.ds(pl.multiple_of(j * rows, rows), rows)

        @pl.when(block_needed)
        def _():
            a, b = mine[:, span], other[:, span]
            lower = jnp.where(upper, b, a)
            above = jnp.where(upper, a, b)
            key_rows = jnp.concatenate([lower[:half, :], above[:half, :]], axis=0)
            value_rows = jnp.concatenate([lower[half:, :], above[half:, :]], axis=0)
            keys_t[...] = key_rows
            keys[...] = key_rows.T
            values[...] = value_rows.T

            def key_tile(index, carry):
                base = pl.multiple_of(index * TILE, TILE)
                key_lo = block_lo + base
                dk[...] = jnp.zeros_like(dk)
                dv[...] = jnp.zeros_like(dv)

                def query_tile(t, inner):
                    query_lo = first_pos + t * TILE
                    least, top = lowest[0], highest[0]
                    for other_t in range(1, tiles):
                        least = jnp.where(t == other_t, lowest[other_t], least)
                        top = jnp.where(t == other_t, highest[other_t], top)
                    needed = (key_lo <= query_lo + TILE - 1) & (key_lo + TILE - 1 >= least)

                    inside = (key_lo + TILE - 1 <= query_lo) & (key_lo >= top)

                    def tile(masked):
                        k = keys[pl.ds(base, TILE), :]
                        v = values[pl.ds(base, TILE), :]
                        kt = keys_t[:, pl.ds(base, TILE)]
                        lanes = pl.ds(pl.multiple_of(t * wide, wide), wide)
                        qs, gs = qt[:, lanes], gt[:, lanes]
                        scores = dot(k, qs) * (scale * LOG2E)
                        probs = jnp.exp2(scores - facts[0:1, lanes])
                        if masked:
                            offset = lax.broadcasted_iota(jnp.int32, (TILE, wide), 0)
                            offset = offset.astype(jnp.float32)
                            shift = key_lo.astype(jnp.float32)
                            allowed = (offset <= facts[3:4, lanes] - shift) & (
                                offset >= facts[2:3, lanes] - shift
                            )
                            probs = jnp.where(allowed, probs, 0.0)
                        dscores = probs * (dot(v, gs) - facts[1:2, lanes])
                        probs = probs.astype(jnp.bfloat16)
                        dscores = dscores.astype(jnp.bfloat16)
                        dv[...] += dot(gs, probs, NT)
                        dk[...] += dot(qs, dscores, NT)
                        dq[:, lanes] += dot(kt, dscores)

                    pl.when(inside)(functools.partial(tile, False))
                    pl.when(needed & jnp.logical_not(inside))(functools.partial(tile, True))

                    return inner

                lax.fori_loop(0, tiles, query_tile, 0)
                key_sum, value_sum = dk[...], dv[...]
                lower = jnp.concatenate([key_sum[:half], value_sum[:half]], axis=0)
                above = jnp.concatenate([key_sum[half:], value_sum[half:]], axis=0)
                out = pl.ds(pl.multiple_of(j * rows + base, TILE), TILE)
                kept[:, out] = jnp.where(upper, above, lower)
                sent[:, out] = jnp.where(upper, lower, above).astype(sent.dtype)
                return carry

            lax.fori_loop(0, tiles, key_tile, 0)

        @pl.when(jnp.logical_not(block_needed))
        def _():
            kept[:, span] = jnp.zeros((size, rows), kept.dtype)
            sent[:, span] = jnp.zeros((size, rows), sent.dtype)

        return state

    lax.fori_loop(0, blocks, block, 0)


def finish_kernel(heads, scale, dq, out):
    rows, size = out.shape[0], dq.shape[0]
    for t in range(rows // TILE):
        for h in range(heads):
            span = slice((t * heads + h) * TILE, (t * heads + h + 1) * TILE)
            out[t * TILE : (t + 1) * TILE, h * size : (h + 1) * size] = (
                (dq[:, span] * scale).astype(out.dtype).T
            )


def finish_call(dq, heads):
    size, rows = dq.shape[0], dq.shape[1] // heads
    vmem = pl.BlockSpec(memory_space=pltpu.VMEM)
    return pl.pallas_call(
        functools.partial(finish_kernel, heads, size ** (-0.5)),
        out_shape=jax.ShapeDtypeStruct((rows, heads * size), jnp.bfloat16),
        in_specs=[vmem],
        out_specs=vmem,
        cost_estimate=pl.CostEstimate(flops=2**31, bytes_accessed=2**20, transcendentals=0),
    )(dq)


def total_kernel(scale, count, total, *rest):
    terms, (keys_out, values_out, keys_v, values_v, sems) = rest[:count], rest[count:]
    half = total.shape[0] // 2
    summed = total[...]
    for term in terms:
        summed = summed + term[...].astype(jnp.float32)
    keys_v[...] = (summed[:half] * scale).astype(keys_v.dtype)
    values_v[...] = summed[half:].astype(values_v.dtype)
    pairs = ((keys_v, keys_out), (values_v, values_out))
    writes = [pltpu.make_async_copy(a, b, sems.at[i]) for i, (a, b) in enumerate(pairs)]
    for write in writes:
        write.start()
    for write in writes:
        write.wait()


def total_call(total, terms, scale):
    size, rows = total.shape
    vmem = pl.BlockSpec(memory_space=pltpu.VMEM)
    return pl.pallas_call(
        functools.partial(total_kernel, scale, len(terms)),
        out_shape=[jax.ShapeDtypeStruct((size // 2, rows), jnp.bfloat16)] * 2,
        in_specs=[vmem] * (len(terms) + 1),
        out_specs=[pl.BlockSpec(memory_space=pltpu.HBM)] * 2,
        scratch_shapes=[pltpu.VMEM((size // 2, rows), jnp.bfloat16)] * 2
        + [pltpu.SemaphoreType.DMA((2,))],
        compiler_params=pltpu.CompilerParams(vmem_limit_bytes=8 * 1024 * 1024),
    )(total, *terms)


def block_call(distances, first, heads, place, docs, q, g, a, b, mine, other):
    if first:
        rows, width = q.shape
    else:
        rows, width = q.shape[1] // heads, q.shape[0] * heads
    size = width // heads
    blocks = len(distances)
    total = blocks * rows
    scale = size ** (-0.5)
    smem = pl.BlockSpec(memory_space=pltpu.SMEM)
    vmem = pl.BlockSpec(memory_space=pltpu.VMEM)
    operands = [q, g, a, b, mine, other]
    outs = [
        jax.ShapeDtypeStruct((size, heads * rows), jnp.float32)
    ]
    if first:
        outs.append(jax.ShapeDtypeStruct((8, heads * rows), jnp.float32))
        outs += [jax.ShapeDtypeStruct((size, heads * rows), jnp.bfloat16)] * 2
    outs += [
        jax.ShapeDtypeStruct((size, total), jnp.float32),
        jax.ShapeDtypeStruct((size, total), jnp.bfloat16),
    ]
    scratch = [
        pltpu.VMEM((rows, size), jnp.bfloat16),
        pltpu.VMEM((size, rows), jnp.bfloat16),
        pltpu.VMEM((rows, size), jnp.bfloat16),
        pltpu.VMEM((size, TILE), jnp.float32),
        pltpu.VMEM((size, TILE), jnp.float32),
    ]
    specs = [smem, smem] + [vmem] * len(operands)
    if first:
        hbm = pl.BlockSpec(memory_space=pltpu.HBM)
        specs = [smem, smem, hbm, hbm, vmem, hbm, vmem, vmem]
        scratch += [pltpu.VMEM((rows, width), jnp.bfloat16)] * 3
        scratch.append(pltpu.SemaphoreType.DMA((3,)))
    return pl.pallas_call(
        functools.partial(block_kernel, distances, first, heads, scale),
        out_shape=outs,
        in_specs=specs,
        out_specs=[vmem] * len(outs),
        scratch_shapes=scratch,
        input_output_aliases={} if first else {5: 0},
        cost_estimate=pl.CostEstimate(
            flops=blocks * 10 * rows * rows * width * 2,
            bytes_accessed=4 * rows * width,
            transcendentals=blocks * heads * rows * rows,
        ),
        compiler_params=pltpu.CompilerParams(vmem_limit_bytes=32 * 1024 * 1024),
    )(place, docs, *operands)


def local(queries, key_states, value_states, attn_out, grad_out, log_norm, doc_lengths):
    rows, half = key_states.shape
    heads = log_norm.shape[0]
    scale = (2 * half) ** (-0.5)
    place = jnp.stack([lax.axis_index("ctx"), lax.axis_index("head") % 2]).astype(jnp.int32)
    own = jnp.concatenate([key_states.T, value_states.T], axis=0)
    own_other = partner(own)
    second, first = passed_along(own, 2), passed_along(own, 1)

    def stage(distances, blocks, others, first=False):
        return block_call(
            distances, first, heads, place, doc_lengths, q, g, facts, dq, blocks, others
        )

    def pair_sum(kept, sent):
        return kept + partner(sent).astype(jnp.float32)

    in_hbm = lambda x: pltpu.with_memory_space_constraint(x, pltpu.HBM)
    q, g, facts, dq = in_hbm(queries), in_hbm(grad_out), log_norm, in_hbm(attn_out)
    dq, facts, q, g, own_kept, own_sent = stage((0,), own, own_other, True)
    second, first, dq = lax.optimization_barrier((second, first, dq))
    near = jnp.concatenate([second, first], axis=1)
    far = passed_along(near, 2)
    total = pair_sum(own_kept, own_sent)
    dq, near_kept, near_sent = stage((2, 1), near, partner(near))
    far, near_sent, dq = lax.optimization_barrier((far, near_sent, dq))
    near_sum = pair_sum(near_kept, near_sent)
    if DIRECT:
        near_terms = near_sum.astype(jnp.bfloat16)
        dq, near_terms = lax.optimization_barrier((dq, near_terms))
        backs = [passed_along(near_terms[:, :rows], -2), passed_along(near_terms[:, rows:], -1)]
        dq, far_kept, far_sent = stage((4, 3), far, partner(far))
        far_sent, backs = lax.optimization_barrier((far_sent, backs))
        far_terms = pair_sum(far_kept, far_sent).astype(jnp.bfloat16)
        backs += [passed_along(far_terms[:, :rows], -4), passed_along(far_terms[:, rows:], -3)]
    else:
        dq, far_kept, far_sent = stage((4, 3), far, partner(far))
        far_terms = pair_sum(far_kept, far_sent).astype(jnp.bfloat16)
        near_sum = near_sum + passed_along(far_terms, -2).astype(jnp.float32)
        near_terms = near_sum.astype(jnp.bfloat16)
        backs = [passed_along(near_terms[:, rows:], -1), passed_along(near_terms[:, :rows], -2)]
    grad_keys, grad_values = total_call(total, backs, scale)
    return finish_call(dq, heads), grad_keys.T, grad_values.T


def solution(mesh):
    in_specs = (
        P("ctx", "head"),
        P("ctx", "head"),
        P("ctx", "head"),
        P("ctx", "head"),
        P("ctx", "head"),
        P("head", "ctx"),
        P(),
    )
    out_specs = (P("ctx", "head"), P("ctx", "head"), P("ctx", "head"))
    return jax.shard_map(local, mesh=mesh, in_specs=in_specs, out_specs=out_specs, check_vma=False)
```

```python
import functools

import jax
import jax.numpy as jnp
from jax import lax
from jax.experimental import pallas as pl
from jax.experimental.pallas import tpu as pltpu
from jax.sharding import PartitionSpec as P

DIRECT = False
TILE = 256
LOG2E = 1.4426950408889634
NN = (((1,), (0,)), ((), ()))
NT = (((1,), (1,)), ((), ()))


def partner(value):
    count = lax.axis_size("head")
    return lax.ppermute(value, "head", [(i, i ^ 1) for i in range(count)])


def passed_along(value, by):
    count = lax.axis_size("ctx")
    return lax.ppermute(value, "ctx", [(i, (i + by) % count) for i in range(count)])


def dot(a, b, dims=NN):
    return lax.dot_general(a, b, dims, preferred_element_type=jnp.float32)


def row_start(docs, position):
    def step(j, state):
        total, found = state
        total = total + docs[j]
        return total, jnp.where(total <= position, total, found)

    zero = jnp.int32(0)
    return lax.fori_loop(0, docs.shape[0], step, (zero, zero), unroll=True)[1]


def row_starts(docs, positions):
    def step(j, state):
        total, found = state
        total = total + docs[j]
        return total, jnp.where(positions >= total, total, found)

    start = (jnp.int32(0), jnp.zeros_like(positions))
    return lax.fori_loop(0, docs.shape[0], step, start, unroll=True)[1]


def prepare_rows(first_pos, docs, g, norms, attn_out, facts, tiles, heads, size):
    rows = tiles * TILE
    positions = first_pos + lax.broadcasted_iota(jnp.int32, (1, rows), 1)
    starts = row_starts(docs, positions).astype(jnp.float32)
    positions = positions.astype(jnp.float32)
    ones = jnp.ones((8, size), jnp.bfloat16)
    for h in range(heads):
        cols = slice(h * size, (h + 1) * size)
        product = attn_out[:, cols].astype(jnp.float32) * g[:, cols].astype(jnp.float32)
        high = product.astype(jnp.bfloat16)
        low = (product - high.astype(jnp.float32)).astype(jnp.bfloat16)
        delta = (dot(ones, high, NT) + dot(ones, low, NT))[:1, :]
        level = norms[h : h + 1, :] * LOG2E
        for t in range(tiles):
            span = slice((t * heads + h) * TILE, (t * heads + h + 1) * TILE)
            part = slice(t * TILE, (t + 1) * TILE)
            facts[0:1, span] = level[:, part]
            facts[1:2, span] = delta[:, part]
            facts[2:3, span] = starts[:, part]
            facts[3:4, span] = positions[:, part]


def block_kernel(distances, first, heads, scale, place, docs, qt, gt, *rest):
    blocks = len(distances)
    rest = list(rest)
    if first:
        norms_hbm, attn_hbm = rest.pop(0), rest.pop(0)
    else:
        facts, prior = rest.pop(0), rest.pop(0)
    mine, other, rest = rest[0], rest[1], rest[2:]
    query_out = rest.pop(0)
    if first:
        facts = rest.pop(0)
        q_hbm, g_hbm, qt, gt = qt, gt, rest.pop(0), rest.pop(0)
    kept, sent, keys, keys_t, values, dk, dv = rest[:7]
    dq = query_out
    if first:
        attn_out, q, g, norms, docs_here, sems = rest[7:]
        pairs = (
            (docs, docs_here),
            (norms_hbm, norms),
            (attn_hbm, attn_out),
            (g_hbm, g),
            (q_hbm, q),
        )
        loads = [pltpu.make_async_copy(a, b, sems.at[i]) for i, (a, b) in enumerate(pairs)]
        for load in loads:
            load.start()
        loads[0].wait()
        docs = docs_here
    size, rows = qt.shape[0], qt.shape[1] // heads
    half = size // 2
    tiles = rows // TILE
    wide = heads * TILE
    ctx_index, upper = place[0], place[1] == 1
    first_pos = ctx_index * rows
    lowest = [row_start(docs, first_pos + t * TILE) for t in range(tiles)]
    highest = [row_start(docs, first_pos + (t + 1) * TILE - 1) for t in range(tiles)]

    if first:
        for load in loads[1:-1]:
            load.wait()
        prepare_rows(first_pos, docs, g, norms, attn_out, facts, tiles, heads, size)
        for t in range(tiles):
            for h in range(heads):
                span = slice((t * heads + h) * TILE, (t * heads + h + 1) * TILE)
                part = slice(t * TILE, (t + 1) * TILE)
                cols = slice(h * size, (h + 1) * size)
                gt[:, span] = g[part, cols].T
        loads[-1].wait()
        for t in range(tiles):
            for h in range(heads):
                span = slice((t * heads + h) * TILE, (t * heads + h + 1) * TILE)
                part = slice(t * TILE, (t + 1) * TILE)
                cols = slice(h * size, (h + 1) * size)
                qt[:, span] = q[part, cols].T
        dq[...] = jnp.zeros_like(dq)

    def block(j, state):
        block_lo = (ctx_index - distances[0] + j) * rows
        block_needed = (block_lo >= 0) & (block_lo + rows > lowest[0])
        span = pl.ds(pl.multiple_of(j * rows, rows), rows)

        @pl.when(block_needed)
        def _():
            a, b = mine[:, span], other[:, span]
            lower = jnp.where(upper, b, a)
            above = jnp.where(upper, a, b)
            key_rows = jnp.concatenate([lower[:half, :], above[:half, :]], axis=0)
            value_rows = jnp.concatenate([lower[half:, :], above[half:, :]], axis=0)
            keys_t[...] = key_rows
            keys[...] = key_rows.T
            values[...] = value_rows.T

            def key_tile(index, carry):
                base = pl.multiple_of(index * TILE, TILE)
                key_lo = block_lo + base
                dk[...] = jnp.zeros_like(dk)
                dv[...] = jnp.zeros_like(dv)

                def query_tile(t, inner):
                    query_lo = first_pos + t * TILE
                    least, top = lowest[0], highest[0]
                    for other_t in range(1, tiles):
                        least = jnp.where(t == other_t, lowest[other_t], least)
                        top = jnp.where(t == other_t, highest[other_t], top)
                    needed = (key_lo <= query_lo + TILE - 1) & (key_lo + TILE - 1 >= least)

                    inside = (key_lo + TILE - 1 <= query_lo) & (key_lo >= top)

                    def tile(masked):
                        k = keys[pl.ds(base, TILE), :]
                        v = values[pl.ds(base, TILE), :]
                        kt = keys_t[:, pl.ds(base, TILE)]
                        lanes = pl.ds(pl.multiple_of(t * wide, wide), wide)
                        qs, gs = qt[:, lanes], gt[:, lanes]
                        scores = dot(k, qs) * (scale * LOG2E)
                        probs = jnp.exp2(scores - facts[0:1, lanes])
                        if masked:
                            offset = lax.broadcasted_iota(jnp.int32, (TILE, wide), 0)
                            offset = offset.astype(jnp.float32)
                            shift = key_lo.astype(jnp.float32)
                            allowed = (offset <= facts[3:4, lanes] - shift) & (
                                offset >= facts[2:3, lanes] - shift
                            )
                            probs = jnp.where(allowed, probs, 0.0)
                        dscores = probs * (dot(v, gs) - facts[1:2, lanes])
                        probs = probs.astype(jnp.bfloat16)
                        dscores = dscores.astype(jnp.bfloat16)
                        dv[...] += dot(gs, probs, NT)
                        dk[...] += dot(qs, dscores, NT)
                        dq[:, lanes] += dot(kt, dscores)

                    pl.when(inside)(functools.partial(tile, False))
                    pl.when(needed & jnp.logical_not(inside))(functools.partial(tile, True))

                    return inner

                lax.fori_loop(0, tiles, query_tile, 0)
                key_sum, value_sum = dk[...], dv[...]
                lower = jnp.concatenate([key_sum[:half], value_sum[:half]], axis=0)
                above = jnp.concatenate([key_sum[half:], value_sum[half:]], axis=0)
                out = pl.ds(pl.multiple_of(j * rows + base, TILE), TILE)
                kept[:, out] = jnp.where(upper, above, lower)
                sent[:, out] = jnp.where(upper, lower, above).astype(sent.dtype)
                return carry

            lax.fori_loop(0, tiles, key_tile, 0)

        @pl.when(jnp.logical_not(block_needed))
        def _():
            kept[:, span] = jnp.zeros((size, rows), kept.dtype)
            sent[:, span] = jnp.zeros((size, rows), sent.dtype)

        return state

    lax.fori_loop(0, blocks, block, 0)


def finish_kernel(heads, scale, dq, out):
    rows, size = out.shape[0], dq.shape[0]
    for t in range(rows // TILE):
        for h in range(heads):
            span = slice((t * heads + h) * TILE, (t * heads + h + 1) * TILE)
            out[t * TILE : (t + 1) * TILE, h * size : (h + 1) * size] = (
                (dq[:, span] * scale).astype(out.dtype).T
            )


def finish_call(dq, heads):
    size, rows = dq.shape[0], dq.shape[1] // heads
    vmem = pl.BlockSpec(memory_space=pltpu.VMEM)
    return pl.pallas_call(
        functools.partial(finish_kernel, heads, size ** (-0.5)),
        out_shape=jax.ShapeDtypeStruct((rows, heads * size), jnp.bfloat16),
        in_specs=[vmem],
        out_specs=vmem,
        cost_estimate=pl.CostEstimate(flops=2**31, bytes_accessed=2**20, transcendentals=0),
    )(dq)


def total_kernel(scale, count, total, *rest):
    terms, (keys_out, values_out, keys_v, values_v, sems) = rest[:count], rest[count:]
    half = total.shape[0] // 2
    summed = total[...]
    for term in terms:
        summed = summed + term[...].astype(jnp.float32)
    keys_v[...] = (summed[:half] * scale).astype(keys_v.dtype)
    values_v[...] = summed[half:].astype(values_v.dtype)
    pairs = ((keys_v, keys_out), (values_v, values_out))
    writes = [pltpu.make_async_copy(a, b, sems.at[i]) for i, (a, b) in enumerate(pairs)]
    for write in writes:
        write.start()
    for write in writes:
        write.wait()


def total_call(total, terms, scale):
    size, rows = total.shape
    vmem = pl.BlockSpec(memory_space=pltpu.VMEM)
    return pl.pallas_call(
        functools.partial(total_kernel, scale, len(terms)),
        out_shape=[jax.ShapeDtypeStruct((size // 2, rows), jnp.bfloat16)] * 2,
        in_specs=[vmem] * (len(terms) + 1),
        out_specs=[pl.BlockSpec(memory_space=pltpu.HBM)] * 2,
        scratch_shapes=[pltpu.VMEM((size // 2, rows), jnp.bfloat16)] * 2
        + [pltpu.SemaphoreType.DMA((2,))],
        compiler_params=pltpu.CompilerParams(vmem_limit_bytes=8 * 1024 * 1024),
    )(total, *terms)


def block_call(distances, first, heads, place, docs, q, g, a, b, mine, other):
    if first:
        rows, width = q.shape
    else:
        rows, width = q.shape[1] // heads, q.shape[0] * heads
    size = width // heads
    blocks = len(distances)
    total = blocks * rows
    scale = size ** (-0.5)
    smem = pl.BlockSpec(memory_space=pltpu.SMEM)
    vmem = pl.BlockSpec(memory_space=pltpu.VMEM)
    operands = [q, g, a, b, mine, other]
    outs = [
        jax.ShapeDtypeStruct((size, heads * rows), jnp.float32)
    ]
    if first:
        outs.append(jax.ShapeDtypeStruct((8, heads * rows), jnp.float32))
        outs += [jax.ShapeDtypeStruct((size, heads * rows), jnp.bfloat16)] * 2
    outs += [
        jax.ShapeDtypeStruct((size, total), jnp.float32),
        jax.ShapeDtypeStruct((size, total), jnp.bfloat16),
    ]
    scratch = [
        pltpu.VMEM((rows, size), jnp.bfloat16),
        pltpu.VMEM((size, rows), jnp.bfloat16),
        pltpu.VMEM((rows, size), jnp.bfloat16),
        pltpu.VMEM((size, TILE), jnp.float32),
        pltpu.VMEM((size, TILE), jnp.float32),
    ]
    specs = [smem, smem] + [vmem] * len(operands)
    if first:
        hbm = pl.BlockSpec(memory_space=pltpu.HBM)
        specs = [smem, hbm, hbm, hbm, hbm, hbm, vmem, vmem]
        scratch += [pltpu.VMEM((rows, width), jnp.bfloat16)] * 3
        scratch += [pltpu.VMEM((heads, rows), jnp.float32), pltpu.SMEM(docs.shape, jnp.int32)]
        scratch.append(pltpu.SemaphoreType.DMA((5,)))
    return pl.pallas_call(
        functools.partial(block_kernel, distances, first, heads, scale),
        out_shape=outs,
        in_specs=specs,
        out_specs=[vmem] * len(outs),
        scratch_shapes=scratch,
        input_output_aliases={} if first else {5: 0},
        cost_estimate=pl.CostEstimate(
            flops=blocks * 10 * rows * rows * width * 2,
            bytes_accessed=4 * rows * width,
            transcendentals=blocks * heads * rows * rows,
        ),
        compiler_params=pltpu.CompilerParams(vmem_limit_bytes=32 * 1024 * 1024),
    )(place, docs, *operands)


def local(queries, key_states, value_states, attn_out, grad_out, log_norm, doc_lengths):
    rows, half = key_states.shape
    heads = log_norm.shape[0]
    scale = (2 * half) ** (-0.5)
    place = jnp.stack([lax.axis_index("ctx"), lax.axis_index("head") % 2]).astype(jnp.int32)
    own = jnp.concatenate([key_states.T, value_states.T], axis=0)
    own_other = partner(own)
    second, first = passed_along(own, 2), passed_along(own, 1)

    def stage(distances, blocks, others, first=False):
        return block_call(
            distances, first, heads, place, in_hbm(doc_lengths) if first else doc_lengths, q, g, facts, dq, blocks, others
        )

    def pair_sum(kept, sent):
        return kept + partner(sent).astype(jnp.float32)

    in_hbm = lambda x: pltpu.with_memory_space_constraint(x, pltpu.HBM)
    q, g, facts, dq = in_hbm(queries), in_hbm(grad_out), in_hbm(log_norm), in_hbm(attn_out)
    dq, facts, q, g, own_kept, own_sent = stage((0,), own, own_other, True)
    second, first, dq = lax.optimization_barrier((second, first, dq))
    near = jnp.concatenate([second, first], axis=1)
    far = passed_along(near, 2)
    total = pair_sum(own_kept, own_sent)
    dq, near_kept, near_sent = stage((2, 1), near, partner(near))
    far, near_sent, dq = lax.optimization_barrier((far, near_sent, dq))
    near_sum = pair_sum(near_kept, near_sent)
    if DIRECT:
        near_terms = near_sum.astype(jnp.bfloat16)
        dq, near_terms = lax.optimization_barrier((dq, near_terms))
        backs = [passed_along(near_terms[:, :rows], -2), passed_along(near_terms[:, rows:], -1)]
        dq, far_kept, far_sent = stage((4, 3), far, partner(far))
        far_sent, backs = lax.optimization_barrier((far_sent, backs))
        far_terms = pair_sum(far_kept, far_sent).astype(jnp.bfloat16)
        backs += [passed_along(far_terms[:, :rows], -4), passed_along(far_terms[:, rows:], -3)]
    else:
        dq, far_kept, far_sent = stage((4, 3), far, partner(far))
        far_terms = pair_sum(far_kept, far_sent).astype(jnp.bfloat16)
        near_sum = near_sum + passed_along(far_terms, -2).astype(jnp.float32)
        near_terms = near_sum.astype(jnp.bfloat16)
        backs = [passed_along(near_terms[:, rows:], -1), passed_along(near_terms[:, :rows], -2)]
    grad_keys, grad_values = total_call(total, backs, scale)
    return finish_call(dq, heads), grad_keys.T, grad_values.T


def solution(mesh):
    in_specs = (
        P("ctx", "head"),
        P("ctx", "head"),
        P("ctx", "head"),
        P("ctx", "head"),
        P("ctx", "head"),
        P("head", "ctx"),
        P(),
    )
    out_specs = (P("ctx", "head"), P("ctx", "head"), P("ctx", "head"))
    return jax.shard_map(local, mesh=mesh, in_specs=in_specs, out_specs=out_specs, check_vma=False)
```
